128 devices in a mesh: dp: 32 (over z, x, y_lo), mp: 4 (over y_hi, core).
Axes of the slice: x: 4, y: 4 (y_hi: 2, y_lo: 2; y = y_hi * 2 + y_lo), z: 4, core: 2. Of those that a mesh axis runs over, the one named last changes fastest.
Arguments:
- tokens: bfloat16 [2, 16384, 5120], P(None, 'dp', 'mp'), may hold values from -6 to 6
- cot_key: bfloat16 [2, 16384, 1024], P(None, ('dp', 'mp')), may hold values from -24 to 24
- cot_value: bfloat16 [2, 16384, 1024], P(None, ('dp', 'mp')), may hold values from -24 to 24
- key_master: float32 [1024, 5120], P('dp', 'mp')
- value_master: float32 [1024, 5120], P('dp', 'mp')
Outputs:
- keys: bfloat16 [2, 16384, 1024], P(None, ('dp', 'mp'))
- values: bfloat16 [2, 16384, 1024], P(None, ('dp', 'mp'))
- input_grad: bfloat16 [2, 16384, 5120], P(None, 'dp', 'mp')
- grad_key: float32 [1024, 5120], P('dp', 'mp')
- grad_value: float32 [1024, 5120], P('dp', 'mp')
The draws below stay inside these ranges and needn't reach their ends.
All inputs are finite; a program needn't handle non-finite values.
Results may differ from the reference program's by a relative error of at most 0.005.
Values may be sent and summed in bfloat16 or wider, within the bound.
A program may use at most 128 MiB of HBM per device.

```python
import math
import jax
import jax.numpy as jnp

D = 5120
KV_DIM = 1024
MICRO = 2
TOKENS = 16384


def master_draw(key):
    first, second = jax.random.split(key)
    base = jax.random.normal(first, (KV_DIM, D), jnp.float32)
    ramp = jnp.exp(math.log(10.0) * jnp.arange(D, dtype=jnp.float32) / (D - 1))
    row_factor = jnp.exp(jax.random.uniform(second, (KV_DIM,), jnp.float32, math.log(0.3), math.log(3.0)))
    return base * ramp[None, :] * row_factor[:, None] / (4.0 * math.sqrt(D))


def draw_key_master(key, part):
    key = jax.random.fold_in(key, 11)
    return master_draw(key)


def draw_value_master(key, part):
    key = jax.random.fold_in(key, 23)
    return master_draw(key)


def spiked(values, key, source, target, shards_of, factor):
    def block_of(axis_at):
        return (jnp.arange(values.shape[axis_at]) // (values.shape[axis_at] // shards_of)).reshape((-1,) + (1,) * (values.ndim - 1 - axis_at))

    one_side = jax.random.permutation(key, shards_of)[block_of(target)]
    far = (block_of(target) + shards_of // 2) % shards_of
    return jnp.where((block_of(source) == one_side) | (block_of(source) == far), factor * values, values)


def level_of(stream_key, shape, cuts, smallest, high):
    def one(position, blocks):
        heights = jax.random.uniform(jax.random.fold_in(jax.random.fold_in(stream_key, 6), position), (blocks,), jnp.float32, smallest / len(cuts), high / len(cuts))
        return jnp.repeat(jnp.exp(heights), shape[position] // blocks).reshape((-1,) + (1,) * (len(shape) - position - 1))

    factor_of = one(*cuts[0])
    for cut in cuts[1:]:
        factor_of = factor_of * one(*cut)
    return factor_of


def gaussian_with(key, shape, deviation, reach, shards, heavy, kind=jnp.bfloat16):
    drawn = deviation * jax.random.normal(key, shape, jnp.float32)
    if shards:
        drawn = drawn * level_of(key, shape, shards, -0.22, 0.18)
    return jnp.clip(spiked(drawn, jax.random.fold_in(key, 3), *heavy), -reach, reach).astype(kind)


def setup_inputs(seed: int = 0) -> dict:
    arg_keys = jax.random.split(jax.random.key(seed), 6)
    return {
        "tokens": gaussian_with(arg_keys[0], (MICRO, TOKENS, D), 1.0, 6.0, ((1, 32), (2, 4)), (2, 1, 32, 2.75)),
        "cot_key": gaussian_with(arg_keys[1], (MICRO, TOKENS, KV_DIM), 1.0, 24.0, ((1, 128),), (1, 2, 128, 5.5)),
        "cot_value": gaussian_with(arg_keys[2], (MICRO, TOKENS, KV_DIM), 1.0, 24.0, ((1, 128),), (1, 2, 128, 5.5)),
        "key_master": draw_key_master(jax.random.fold_in(arg_keys[5], 71), 0),
        "value_master": draw_value_master(jax.random.fold_in(arg_keys[5], 71), 0),
    }


def binarize(master):
    scale = jnp.sum(jnp.abs(master), axis=1) / master.shape[1]
    return (jnp.sign(master) * scale[:, None]).astype(jnp.bfloat16)


def reference(tokens, cot_key, cot_value, key_master, value_master):
    bin_key = binarize(key_master)
    bin_value = binarize(value_master)
    both_weights = jnp.concatenate([bin_key, bin_value], axis=0)
    key_list = []
    value_list = []
    input_list = []
    grad_key = jnp.zeros(key_master.shape, jnp.float32)
    grad_value = jnp.zeros(value_master.shape, jnp.float32)
    for micro in range(MICRO):
        inputs = tokens[micro]
        summed = jnp.dot(inputs, both_weights.T, preferred_element_type=jnp.float32)
        projected = summed.astype(jnp.bfloat16)
        key_list.append(projected[:, :KV_DIM])
        value_list.append(projected[:, KV_DIM:])
        cot_both = jnp.concatenate([cot_key[micro], cot_value[micro]], axis=1)
        input_list.append(jnp.dot(cot_both, both_weights, preferred_element_type=jnp.float32).astype(jnp.bfloat16))
        grad_key = grad_key + jnp.dot(cot_key[micro].T, inputs, preferred_element_type=jnp.float32)
        grad_value = grad_value + jnp.dot(cot_value[micro].T, inputs, preferred_element_type=jnp.float32)
    return (jnp.stack(key_list), jnp.stack(value_list), jnp.stack(input_list), grad_key, grad_value)
```

```python
import functools

import jax
import jax.numpy as jnp
from jax import lax
from jax.experimental import pallas as pl
from jax.experimental.pallas import tpu as pltpu
from jax.sharding import PartitionSpec as P

MESH = pl.DeviceIdType.MESH
F32 = jnp.float32
BF16 = jnp.bfloat16
N_LOCAL = 16
N_SEM = 112


def kernel(
    tok_hbm, ck_hbm, cv_hbm, mk_hbm, mv_hbm,
    keys_hbm, vals_hbm, ig_hbm, gk_hbm, gv_hbm,
    tok, ck, cv, ckt, cvt, mast, sums, wk, wv, part,
    g32, stage, fwd, back, small_out, small_in, yl_out, yl_in, g_out,
    ps_out, ps_in, p_own, y_out, y_in, kv_out, ig,
    lsem, ssem, rsem,
):
    feat = tok.shape[-1]
    feat_all = feat * 4
    dp, mp = lax.axis_index("dp"), lax.axis_index("mp")
    z, x, yl = dp // 8, (dp // 2) % 4, dp % 2
    yh, c = mp // 2, mp % 2

    def dev(z, x, yl, yh, c):
        return ((z * 4 + x) * 2 + yl, yh * 2 + c)

    zs = {"0": z, "p": (z + 1) % 4, "m": (z + 3) % 4, "2": (z + 2) % 4}
    xs = {"0": x, "p": (x + 1) % 4, "m": (x + 3) % 4, "2": (x + 2) % 4}
    z_dev = {n: dev(zs[n], x, yl, yh, c) for n in "pm2"}
    x_dev = {n: dev(z, xs[n], yl, yh, c) for n in "pm2"}
    sib = dev(z, x, yl, yh, 1 - c)
    yl_dev = dev(z, x, 1 - yl, yh, c)
    yh_dev = dev(z, x, yl, 1 - yh, c)
    yh_sib = dev(z, x, yl, 1 - yh, 1 - c)
    peers = [sib, yl_dev, yh_dev, yh_sib] + list(z_dev.values()) + list(x_dev.values())

    ids = {}
    started = []

    def sem_of(name):
        return ids.setdefault(name, len(ids))

    def send(name, src, dst, device):
        k = sem_of(name)
        copy = pltpu.make_async_remote_copy(
            src_ref=src, dst_ref=dst, send_sem=ssem.at[k], recv_sem=rsem.at[k],
            device_id=device, device_id_type=MESH,
        )
        copy.start()
        started.append(copy)

    def arrived(name, ref):
        pltpu.make_async_copy(ref, ref, rsem.at[sem_of(name)]).wait()

    local_ids = []

    def local(src, dst):
        copy = pltpu.make_async_copy(src, dst, lsem.at[len(local_ids)])
        local_ids.append(copy)
        copy.start()
        return copy

    barrier = pltpu.get_barrier_semaphore()
    for peer in peers:
        pl.semaphore_signal(barrier, inc=1, device_id=peer, device_id_type=MESH)
    load_m = [local(mk_hbm, mast.at[0]), local(mv_hbm, mast.at[1])]
    load_c = {"k": local(ck_hbm, ck.at[:, mp]), "v": local(cv_hbm, cv.at[:, mp])}
    load_t = local(tok_hbm, tok)

    for copy in load_m:
        copy.wait()
    acc = jnp.abs(mast[:, :, 0:128])
    for i in range(1, feat // 128):
        acc = acc + jnp.abs(mast[:, :, i * 128 : (i + 1) * 128])
    sums[mp] = acc
    pl.semaphore_wait(barrier, len(peers))
    for name, device in (("sib", sib), ("yh", yh_dev), ("yhs", yh_sib)):
        send("sc_" + name, sums.at[mp], sums.at[mp], device)
    cots = {"k": (ck, ck_hbm, ckt), "v": (cv, cv_hbm, cvt)}

    def send_cot(w):
        full, own, _ = cots[w]
        send("c_yh" + w, own, full.at[:, mp], yh_dev)
        send("c_sib" + w, own, full.at[:, mp], sib)

    send_cot("k")
    slot = {"sib": yh * 2 + 1 - c, "yh": (1 - yh) * 2 + c, "yhs": (1 - yh) * 2 + 1 - c}
    for name in ("sib", "yh", "yhs"):
        arrived("sc_" + name, sums.at[slot[name]])
    total = sums[0] + sums[1] + sums[2] + sums[3]
    scale = jnp.sum(total, axis=-1, keepdims=True) / feat_all

    W = {"k": wk, "v": wv}
    big = {"k": zs, "v": xs}
    minor = {"k": xs, "v": zs}
    big_dev = {"k": z_dev, "v": x_dev}
    minor_dev = {"k": x_dev, "v": z_dev}

    def blk(buf, w, b, j):
        return buf.at[b, j] if w == "k" else buf.at[j, b]

    def own_rows(h):
        return pl.ds(pl.multiple_of((yl if h == "own" else 1 - yl) * 32, 32), 32)

    for i, w in enumerate("kv"):
        m = mast[i]
        sgn = jnp.where(m > 0, 1.0, jnp.where(m < 0, -1.0, 0.0))
        W[w][z, x, own_rows("own")] = (sgn * scale[i]).astype(BF16)

    def small_send(w, h):
        at = W[w].at[z, x, own_rows(h)]
        for n in "pm2":
            send("w" + w + "s" + n + h, at, at, minor_dev[w][n])

    def big_send(w, j):
        at = blk(W[w], w, big[w]["0"], minor[w][j])
        for n in "pm":
            send("w" + w + "b" + n + j, at, at, big_dev[w][n])

    opp = {"p": "m", "m": "p", "2": "2"}

    def small_wait(w, j):
        for h in ("own", "par"):
            arrived("w" + w + "s" + opp[j] + h, blk(W[w], w, big[w]["0"], minor[w][j]).at[own_rows(h)])

    def relay(w, n, j):
        at = blk(W[w], w, big[w][opp[n]], minor[w][j])
        arrived("w" + w + "b" + n + j, at)
        if j in RELAYED[n]:
            send("w" + w + "r" + n + j, at, at, big_dev[w][n])

    def relay_wait(w, n, j):
        arrived("w" + w + "r" + n + j, blk(W[w], w, big[w]["2"], minor[w][j]))

    RELAYED = {"p": "0p", "m": "m2"}

    for w in "kv":
        at = W[w].at[z, x, own_rows("own")]
        send("w" + w + "y", at, at, yl_dev)
    for w in "kv":
        small_send(w, "own")
    for w in "kv":
        arrived("w" + w + "y", W[w].at[z, x, own_rows("par")])
        small_send(w, "par")
    for w in "kv":
        big_send(w, "0")

    def relay_cot(w):
        full = cots[w][0]
        arrived("c_yh" + w, full.at[:, slot["yh"]])
        send("c_r" + w, full.at[:, slot["yh"]], full.at[:, slot["yh"]], sib)

    def all_cots(w):
        full, _, flat = cots[w]
        load_c[w].wait()
        arrived("c_sib" + w, full.at[:, slot["sib"]])
        arrived("c_r" + w, full.at[:, slot["yhs"]])

    def transpose(w):
        full, _, flat = cots[w]

        def one(i, _):
            m, s = i // 4, i % 4
            block = full[m, s]
            at = pl.ds(pl.multiple_of(i * 128, 128), 128)
            flat[:, at] = block.T
            return 0

        lax.fori_loop(0, 8, one, 0)

    G = {"k": 0, "v": 1}

    def grad_chunk(w, zc):
        lhs = cots[w][2][pl.ds(pl.multiple_of(zc * 256, 256), 256), :]

        def one(i, _):
            at = pl.ds(pl.multiple_of(i * 256, 256), 256)
            rhs = tok[:, :, at].reshape(1024, 256)
            res = jnp.dot(lhs, rhs, preferred_element_type=F32)
            g32[G[w], zc, :, :, at] = res.reshape(4, 64, 256)
            return 0

        lax.fori_loop(0, feat // 256, one, 0)

    spots = {"0": 0, "m": 1, "p": 2, "2": 3}
    fwd_spot = {"p": {"0": 0, "p": 1}, "m": {"m": 0, "2": 1}}

    def stage_of(w, b, j):
        return blk(stage.at[G[w]], w, big[w][b], minor[w][j])

    def g_of(w, b, j):
        return blk(g32.at[G[w]], w, big[w][b], minor[w][j])

    def g_far(w, j):
        n = "p" if j in RELAYED["p"] else "m"
        at = stage_of(w, "2", j)
        at[...] = g_of(w, "2", j)[...].astype(BF16)
        send("g" + w + "f" + n + j, at, fwd.at[G[w], 0 if n == "p" else 1, fwd_spot[n][j]], big_dev[w][n])

    def g_near(w, n, j):
        at = stage_of(w, n, j)
        value = g_of(w, n, j)[...]
        if j in RELAYED[n]:
            got = fwd.at[G[w], 0 if n == "p" else 1, fwd_spot[n][j]]
            arrived("g" + w + "f" + n + j, got)
            value = value + got[...].astype(F32)
        at[...] = value.astype(BF16)
        send("g" + w + "b" + n + j, at, back.at[G[w], 0 if n == "p" else 1, spots[j]], big_dev[w][n])

    def g_sum(w, j):
        value = g_of(w, "0", j)[...]
        for i, n in enumerate("pm"):
            got = back.at[G[w], i, spots[j]]
            arrived("g" + w + "b" + n + j, got)
            value = value + got[...].astype(F32)
        if j == "0":
            g_of(w, "0", j)[...] = value
        else:
            at = small_out.at[G[w], spots[j] - 1]
            at[...] = value.astype(BF16)
            send("g" + w + "s" + j, at, small_in.at[G[w], spots[j] - 1], minor_dev[w][j])

    def g_minor(w):
        at = g_of(w, "0", "0")
        value = at[...]
        for j in "mp2":
            got = small_in.at[G[w], spots[j] - 1]
            arrived("g" + w + "s" + j, got)
            value = value + got[...].astype(F32)
        at[...] = value
        yl_out[G[w]] = at[own_rows("par")].astype(BF16)
        send("g" + w + "y", yl_out.at[G[w]], yl_in.at[G[w]], yl_dev)

    def g_last(w, out):
        arrived("g" + w + "y", yl_in.at[G[w]])
        g_out[G[w]] = g_of(w, "0", "0")[own_rows("own")] + yl_in[G[w]].astype(F32)
        return local(g_out.at[G[w]], out)

    def proj(w, zc, q):
        rhs = W[w][zc].reshape(256, feat)

        def one(m, _):
            res = lax.dot_general(tok[m], rhs, (((1,), (1,)), ((), ())), preferred_element_type=F32)
            part[m] = res.reshape(4, 128, 256)
            return 0

        lax.fori_loop(0, 2, one, 0)
        for h in range(2):
            ps_out[q, h] = part[:, h * 2 + 1 - c].astype(BF16)
        send("ps%d" % q, ps_out.at[q], ps_in.at[q], sib)
        p_own[q, 0] = part[:, mp]
        p_own[q, 1] = part[:, (1 - yh) * 2 + c]

    def proj_cross(q):
        arrived("ps%d" % q, ps_in.at[q])
        y_out[q] = (p_own[q, 1] + ps_in[q, 1 - yh].astype(F32)).astype(BF16)
        send("py%d" % q, y_out.at[q], y_in.at[q], yh_dev)

    def proj_last(w, zc, q):
        arrived("py%d" % q, y_in.at[q])
        value = p_own[q, 0] + ps_in[q, yh].astype(F32) + y_in[q].astype(F32)
        kv_out[G[w], :, :, pl.ds(pl.multiple_of(zc * 256, 256), 256)] = value.astype(BF16)

    def input_grad():
        def one(i, _):
            m, n = i // 5, i % 5
            at = pl.ds(pl.multiple_of(n * 256, 256), 256)
            res = jnp.dot(ck[m].reshape(512, 1024), wk[:, :, :, at].reshape(1024, 256), preferred_element_type=F32)
            res = res + jnp.dot(cv[m].reshape(512, 1024), wv[:, :, :, at].reshape(1024, 256), preferred_element_type=F32)
            ig[m, :, at] = res.astype(BF16)
            return 0

        lax.fori_loop(0, 10, one, 0)

    load_t.wait()
    for j in "mp2":
        for w in "kv":
            small_wait(w, j)
            big_send(w, j)
    proj("k", zs["0"], 0)
    relay_cot("k")
    send_cot("v")
    proj_cross(0)
    for w in "kv":
        relay(w, "p", "0")
        relay(w, "m", "m")
    all_cots("k")
    transpose("k")
    for b in "2pm0":
        grad_chunk("k", zs[b])
        if b == "2":
            for j in "m0p2":
                g_far("k", j)
        if b == "p":
            for j in "2m":
                g_near("k", "p", j)
        if b == "m":
            for j in "p0":
                g_near("k", "m", j)
    for w in "kv":
        relay(w, "p", "p")
        relay(w, "m", "2")
    relay_cot("v")
    for j in "m2":
        relay("k", "p", j)
    for j in "0p":
        relay("k", "m", j)
    proj("k", zs["p"], 1)
    proj("k", zs["m"], 2)
    proj_cross(1)
    proj_cross(2)
    all_cots("v")
    transpose("v")
    for b in "2pm0":
        grad_chunk("v", zs[b])
    for j in "m0p2":
        g_far("v", j)
    for j in "2m":
        g_near("v", "p", j)
    for j in "p0":
        g_near("v", "m", j)
    for j in "m2":
        relay("v", "p", j)
    for j in "0p":
        relay("v", "m", j)
    for w in "kv":
        for n in "pm":
            for j in RELAYED[n]:
                relay_wait(w, n, j)
    for j in "0p":
        g_near("k", "p", j)
    for j in "m2":
        g_near("k", "m", j)
    proj("k", zs["2"], 3)
    for i in range(4):
        proj("v", i, 4 + i)
        proj_cross(3 + i)
    proj_cross(7)
    for j in "0p":
        g_near("v", "p", j)
    for j in "m2":
        g_near("v", "m", j)
    input_grad()
    outs = [local(ig, ig_hbm)]
    for w in "kv":
        for j in "2pm0":
            g_sum(w, j)
    for w in "kv":
        g_minor(w)
    for i, b in enumerate("0pm2"):
        proj_last("k", zs[b], i)
    outs.append(local(kv_out.at[0], keys_hbm))
    for i in range(4):
        proj_last("v", i, 4 + i)
    outs.append(local(kv_out.at[1], vals_hbm))
    outs.append(g_last("k", gk_hbm))
    outs.append(g_last("v", gv_hbm))
    for copy in outs:
        copy.wait()
    assert len(ids) <= N_SEM and len(local_ids) <= N_LOCAL
    for copy in started:
        copy.wait_send()


def per_device(tokens, cot_key, cot_value, key_master, value_master):
    feat = tokens.shape[2]
    rows = key_master.shape[0]
    any_spec = pl.BlockSpec(memory_space=pl.ANY)
    vmem = pltpu.VMEM
    return pl.pallas_call(
        kernel,
        out_shape=(
            jax.ShapeDtypeStruct(cot_key.shape, BF16),
            jax.ShapeDtypeStruct(cot_value.shape, BF16),
            jax.ShapeDtypeStruct(tokens.shape, BF16),
            jax.ShapeDtypeStruct(key_master.shape, F32),
            jax.ShapeDtypeStruct(value_master.shape, F32),
        ),
        in_specs=[any_spec] * 5,
        out_specs=(any_spec,) * 5,
        scratch_shapes=[
            vmem((2, 512, feat), BF16),
            vmem((2, 4, 128, 1024), BF16),
            vmem((2, 4, 128, 1024), BF16),
            vmem((1024, 1024), BF16),
            vmem((1024, 1024), BF16),
            vmem((2, rows, feat), F32),
            vmem((4, 2, rows, 128), F32),
            vmem((4, 4, 64, feat), BF16),
            vmem((4, 4, 64, feat), BF16),
            vmem((2, 4, 128, 256), F32),
            vmem((2, 4, 4, 64, feat), F32),
            vmem((2, 4, 4, 64, feat), BF16),
            vmem((2, 2, 2, 64, feat), BF16),
            vmem((2, 2, 4, 64, feat), BF16),
            vmem((2, 3, 64, feat), BF16),
            vmem((2, 3, 64, feat), BF16),
            vmem((2, 32, feat), BF16),
            vmem((2, 32, feat), BF16),
            vmem((2, 32, feat), F32),
            vmem((8, 2, 2, 128, 256), BF16),
            vmem((8, 2, 2, 128, 256), BF16),
            vmem((8, 2, 2, 128, 256), F32),
            vmem((8, 2, 128, 256), BF16),
            vmem((8, 2, 128, 256), BF16),
            vmem((2, 2, 128, 1024), BF16),
            vmem((2, 512, feat), BF16),
            pltpu.SemaphoreType.DMA((N_LOCAL,)),
            pltpu.SemaphoreType.DMA((N_SEM,)),
            pltpu.SemaphoreType.DMA((N_SEM,)),
        ],
        compiler_params=pltpu.CompilerParams(
            collective_id=0, has_side_effects=True, vmem_limit_bytes=60 * 2**20
        ),
        cost_estimate=pl.CostEstimate(flops=16 * 10**9, bytes_accessed=10**7, transcendentals=0),
    )(tokens, cot_key, cot_value, key_master, value_master)


def solution(mesh):
    in_specs = (
        P(None, "dp", "mp"),
        P(None, ("dp", "mp"), None),
        P(None, ("dp", "mp"), None),
        P("dp", "mp"),
        P("dp", "mp"),
    )
    out_specs = (
        P(None, ("dp", "mp"), None),
        P(None, ("dp", "mp"), None),
        P(None, "dp", "mp"),
        P("dp", "mp"),
        P("dp", "mp"),
    )
    return jax.shard_map(
        per_device, mesh=mesh, in_specs=in_specs, out_specs=out_specs, check_vma=False
    )
```

```python
import functools

import jax
import jax.numpy as jnp
from jax import lax
from jax.experimental import pallas as pl
from jax.experimental.pallas import tpu as pltpu
from jax.sharding import PartitionSpec as P

MESH = pl.DeviceIdType.MESH
F32 = jnp.float32
BF16 = jnp.bfloat16
N_LOCAL = 16
N_SEM = 112


def kernel(
    tok_hbm, ck_hbm, cv_hbm, mk_hbm, mv_hbm,
    keys_hbm, vals_hbm, ig_hbm, gk_hbm, gv_hbm,
    tok, ck, cv, ckt, cvt, mast, sums, wk, wv, part,
    g32, fwd_out, fwd_in, back_out, back_in, small_out, small_in, g_tot, yl_out, yl_in, g_out,
    ps_out, ps_in, p_own, y_out, y_in, kv_out, ig,
    s_own, s_yl, s_minor, s_full, s_col,
    lsem, ssem, rsem,
):
    feat = tok.shape[-1]
    feat_all = feat * 4
    dp, mp = lax.axis_index("dp"), lax.axis_index("mp")
    z, x, yl = dp // 8, (dp // 2) % 4, dp % 2
    yh, c = mp // 2, mp % 2

    def dev(z, x, yl, yh, c):
        return ((z * 4 + x) * 2 + yl, yh * 2 + c)

    zs = {"0": z, "p": (z + 1) % 4, "m": (z + 3) % 4, "2": (z + 2) % 4}
    xs = {"0": x, "p": (x + 1) % 4, "m": (x + 3) % 4, "2": (x + 2) % 4}
    z_dev = {n: dev(zs[n], x, yl, yh, c) for n in "pm2"}
    x_dev = {n: dev(z, xs[n], yl, yh, c) for n in "pm2"}
    sib = dev(z, x, yl, yh, 1 - c)
    yl_dev = dev(z, x, 1 - yl, yh, c)
    yh_dev = dev(z, x, yl, 1 - yh, c)
    yh_sib = dev(z, x, yl, 1 - yh, 1 - c)
    peers = [sib, yl_dev, yh_dev, yh_sib] + list(z_dev.values()) + list(x_dev.values())

    ids = {}
    started = []

    def sem_of(name):
        return ids.setdefault(name, len(ids))

    def send(name, src, dst, device):
        k = sem_of(name)
        copy = pltpu.make_async_remote_copy(
            src_ref=src, dst_ref=dst, send_sem=ssem.at[k], recv_sem=rsem.at[k],
            device_id=device, device_id_type=MESH,
        )
        copy.start()
        started.append(copy)

    def arrived(name, ref):
        pltpu.make_async_copy(ref, ref, rsem.at[sem_of(name)]).wait()

    local_ids = []

    def local(src, dst):
        copy = pltpu.make_async_copy(src, dst, lsem.at[len(local_ids)])
        local_ids.append(copy)
        copy.start()
        return copy

    barrier = pltpu.get_barrier_semaphore()
    for peer in peers:
        pl.semaphore_signal(barrier, inc=1, device_id=peer, device_id_type=MESH)
    load_m = [local(mk_hbm, mast.at[0]), local(mv_hbm, mast.at[1])]
    load_c = {"k": local(ck_hbm, ck.at[:, mp]), "v": local(cv_hbm, cv.at[:, mp])}
    load_t = local(tok_hbm, tok)

    for copy in load_m:
        copy.wait()

    def partial_sums():
        acc = jnp.abs(mast[:, :, 0:128])
        for i in range(1, feat // 128):
            acc = acc + jnp.abs(mast[:, :, i * 128 : (i + 1) * 128])
        sums[mp] = acc

    def send_sums():
        for name, device in (("sib", sib), ("yh", yh_dev), ("yhs", yh_sib)):
            send("sc_" + name, sums.at[mp], sums.at[mp], device)

    slot = {"sib": yh * 2 + 1 - c, "yh": (1 - yh) * 2 + c, "yhs": (1 - yh) * 2 + 1 - c}

    def own_scale():
        for name in ("sib", "yh", "yhs"):
            arrived("sc_" + name, sums.at[slot[name]])
        total = sums[0] + sums[1] + sums[2] + sums[3]
        scale = jnp.sum(total, axis=-1, keepdims=True) / feat_all
        row = lax.broadcasted_iota(jnp.int32, (32, 256), 0)
        lane = lax.broadcasted_iota(jnp.int32, (32, 256), 1)
        at_home = lane == row + (x * 2 + yl) * 32
        lines = [jnp.sum(jnp.where(at_home, scale[i], 0.0), axis=0, keepdims=True) for i in range(2)]
        s_own[...] = jnp.concatenate(lines + [jnp.zeros((6, 256), F32)], axis=0)
        send("s_yl", s_own, s_yl, yl_dev)

    def row_scales():
        arrived("s_yl", s_yl)
        s_minor[x] = s_own[...] + s_yl[...]
        for n in "pm2":
            send("s_x" + n, s_minor.at[x], s_minor.at[x], x_dev[n])

    def plane_scales():
        for n in "pm2":
            arrived("s_x" + opp[n], s_minor.at[xs[n]])
        s_full[z] = s_minor[0] + s_minor[1] + s_minor[2] + s_minor[3]
        for n in "pm2":
            send("s_z" + n, s_full.at[z], s_full.at[z], z_dev[n])

    def all_scales():
        for n in "pm2":
            arrived("s_z" + opp[n], s_full.at[zs[n]])
        row = lax.broadcasted_iota(jnp.int32, (256, 256), 0)
        lane = lax.broadcasted_iota(jnp.int32, (256, 256), 1)
        for i in range(2):
            for zc in range(4):
                line = s_full[zc, i : i + 1, :]
                column = jnp.sum(jnp.where(row == lane, line, 0.0), axis=1, keepdims=True)
                s_col[i, zc * 256 : (zc + 1) * 256, :] = jnp.broadcast_to(column, (256, 256)).astype(BF16)

    cots = {"k": (ck, ck_hbm, ckt), "v": (cv, cv_hbm, cvt)}

    def send_cot(w):
        full, own, _ = cots[w]
        send("c_yh" + w, own, full.at[:, mp], yh_dev)

    def send_cot_sib(w):
        full, own, _ = cots[w]
        send("c_sib" + w, own, full.at[:, mp], sib)

    W = {"k": wk, "v": wv}
    big = {"k": zs, "v": xs}
    minor = {"k": xs, "v": zs}
    big_dev = {"k": z_dev, "v": x_dev}
    minor_dev = {"k": x_dev, "v": z_dev}

    def blk(buf, w, b, j):
        return buf.at[b, j] if w == "k" else buf.at[j, b]

    def own_rows(h):
        return pl.ds(pl.multiple_of((yl if h == "own" else 1 - yl) * 32, 32), 32)

    for i, w in enumerate("kv"):
        m = mast[i]
        W[w][z, x, own_rows("own")] = jnp.where(m > 0, 1.0, jnp.where(m < 0, -1.0, 0.0)).astype(BF16)

    def small_send(w, h):
        at = W[w].at[z, x, own_rows(h)]
        for n in "pm2":
            send("w" + w + "s" + n + h, at, at, minor_dev[w][n])

    def big_first(w, h):
        at = W[w].at[z, x, own_rows(h)]
        for n in "pm":
            send("w" + w + "b" + n + "0" + h, at, at, big_dev[w][n])

    def big_send(w, j):
        at = blk(W[w], w, big[w]["0"], minor[w][j])
        for n in "pm":
            send("w" + w + "b" + n + j, at, at, big_dev[w][n])

    opp = {"p": "m", "m": "p", "2": "2"}

    def small_wait(w, j):
        for h in ("own", "par"):
            arrived("w" + w + "s" + opp[j] + h, blk(W[w], w, big[w]["0"], minor[w][j]).at[own_rows(h)])

    def relay(w, n, j):
        at = blk(W[w], w, big[w][opp[n]], minor[w][j])
        if j == "0":
            for h in ("own", "par"):
                arrived("w" + w + "b" + n + j + h, at.at[own_rows(h)])
        else:
            arrived("w" + w + "b" + n + j, at)
        if j in RELAYED[n]:
            send("w" + w + "r" + n + j, at, at, big_dev[w][n])

    def relay_wait(w, n, j):
        arrived("w" + w + "r" + n + j, blk(W[w], w, big[w]["2"], minor[w][j]))

    RELAYED = {"p": "0p", "m": "m2"}

    def relay_cot(w):
        full = cots[w][0]
        arrived("c_yh" + w, full.at[:, slot["yh"]])
        send("c_r" + w, full.at[:, slot["yh"]], full.at[:, slot["yh"]], sib)

    def all_cots(w):
        full, _, flat = cots[w]
        load_c[w].wait()
        arrived("c_sib" + w, full.at[:, slot["sib"]])
        arrived("c_r" + w, full.at[:, slot["yhs"]])

    def transpose(w):
        full, _, flat = cots[w]

        def one(i, _):
            m, s = i // 4, i % 4
            block = full[m, s]
            at = pl.ds(pl.multiple_of(i * 128, 128), 128)
            flat[:, at] = block.T
            return 0

        lax.fori_loop(0, 8, one, 0)

    G = {"k": 0, "v": 1}

    def grads(w):
        def one(i, _):
            at = pl.ds(pl.multiple_of(i * 256, 256), 256)
            rhs = tok[:, :, at].reshape(1024, 256)
            res = jnp.dot(cots[w][2][...], rhs, preferred_element_type=F32)
            g32[G[w], :, :, :, at] = res.reshape(4, 4, 64, 256)
            return 0

        lax.fori_loop(0, feat // 256, one, 0)

    g_big, g_small = (zs, xs), (xs, zs)
    g_big_dev, g_small_dev = (z_dev, x_dev), (x_dev, z_dev)
    far = {"p": "0p", "m": "m2"}
    spot = {"p": "2mp0", "m": "p02m"}

    def g_of(w, h, b, j):
        rows = pl.ds(h * 32, 32)
        if h == 0:
            return g32.at[G[w], zs[b], xs[j], rows]
        return g32.at[G[w], zs[j], xs[b], rows]

    def g_far(w, h):
        for d, n in enumerate("pm"):
            at = fwd_out.at[G[w], h, d]
            for i, j in enumerate(far[n]):
                at[i] = g_of(w, h, "2", j)[...].astype(BF16)
            send("gf%s%d%s" % (w, h, n), at, fwd_in.at[G[w], h, d], g_big_dev[h][n])

    def g_near(w, h):
        for d, n in enumerate("pm"):
            for i in range(2):
                back_out[G[w], h, d, i] = g_of(w, h, n, spot[n][i])[...].astype(BF16)
            at = pl.ds(0, 2)
            send("gb%s%d%s" % (w, h, n), back_out.at[G[w], h, d, at], back_in.at[G[w], h, d, at], g_big_dev[h][n])

    def g_relay(w, h):
        for d, n in enumerate("pm"):
            got = fwd_in.at[G[w], h, d]
            arrived("gf%s%d%s" % (w, h, n), got)
            for i in range(2, 4):
                j = spot[n][i]
                value = g_of(w, h, n, j)[...] + got[far[n].index(j)].astype(F32)
                back_out[G[w], h, d, i] = value.astype(BF16)
            at = pl.ds(2, 2)
            send("gr%s%d%s" % (w, h, n), back_out.at[G[w], h, d, at], back_in.at[G[w], h, d, at], g_big_dev[h][n])

    def g_sum(w, h):
        for d, n in enumerate("pm"):
            arrived("gb%s%d%s" % (w, h, n), back_in.at[G[w], h, d, pl.ds(0, 2)])
            arrived("gr%s%d%s" % (w, h, n), back_in.at[G[w], h, d, pl.ds(2, 2)])
        for i, j in enumerate("2pm0"):
            value = g_of(w, h, "0", j)[...]
            for d, n in enumerate("pm"):
                value = value + back_in[G[w], h, d, spot[n].index(j)].astype(F32)
            if j == "0":
                g_tot[G[w], h] = value
            else:
                small_out[G[w], h, i] = value.astype(BF16)
                send("gs%s%d%s" % (w, h, j), small_out.at[G[w], h, i], small_in.at[G[w], h, i], g_small_dev[h][j])

    def g_minor(w):
        for h in range(2):
            value = g_tot[G[w], h]
            for i, j in enumerate("2pm"):
                got = small_in.at[G[w], h, i]
                arrived("gs%s%d%s" % (w, h, j), got)
                value = value + got[...].astype(F32)
            g_tot[G[w], h] = value
        yl_out[G[w]] = g_tot[G[w], 1 - yl].astype(BF16)
        send("g" + w + "y", yl_out.at[G[w]], yl_in.at[G[w]], yl_dev)

    def g_last(w, out):
        arrived("g" + w + "y", yl_in.at[G[w]])
        g_out[G[w]] = g_tot[G[w], yl] + yl_in[G[w]].astype(F32)
        store(g_out.at[G[w]], out)

    def proj(w, zc, q):
        rhs = W[w][zc].reshape(256, feat)

        def one(m, _):
            res = lax.dot_general(tok[m], rhs, (((1,), (1,)), ((), ())), preferred_element_type=F32)
            part[m] = res.reshape(4, 128, 256)
            return 0

        lax.fori_loop(0, 2, one, 0)
        for h in range(2):
            ps_out[q, h] = part[:, h * 2 + 1 - c].astype(BF16)
        send("ps%d" % q, ps_out.at[q], ps_in.at[q], sib)
        p_own[q, 0] = part[:, mp]
        p_own[q, 1] = part[:, (1 - yh) * 2 + c]

    def proj_cross(q):
        arrived("ps%d" % q, ps_in.at[q])
        y_out[q] = (p_own[q, 1] + ps_in[q, 1 - yh].astype(F32)).astype(BF16)
        send("py%d" % q, y_out.at[q], y_in.at[q], yh_dev)

    def proj_last(w, zc, q):
        arrived("py%d" % q, y_in.at[q])
        line = s_full[zc, G[w] : G[w] + 1, :].astype(BF16).astype(F32)
        value = (p_own[q, 0] + ps_in[q, yh].astype(F32) + y_in[q].astype(F32)) * line
        kv_out[G[w], :, :, pl.ds(pl.multiple_of(zc * 256, 256), 256)] = value.astype(BF16)

    def input_grad():
        def one(n, _):
            at = pl.ds(pl.multiple_of(n * 256, 256), 256)
            wide_k = wk[:, :, :, at].reshape(1024, 256) * s_col[0]
            wide_v = wv[:, :, :, at].reshape(1024, 256) * s_col[1]
            for m in range(2):
                res = jnp.dot(ck[m].reshape(512, 1024), wide_k, preferred_element_type=F32)
                res = res + jnp.dot(cv[m].reshape(512, 1024), wide_v, preferred_element_type=F32)
                ig[m, :, at] = res.astype(BF16)
            return 0

        lax.fori_loop(0, feat // 256, one, 0)

    outs = []

    def store(src, dst):
        outs.append(local(src, dst))

    def step(what, *todo):
        with jax.named_scope(what):
            for fn, *args in todo:
                fn(*args)

    def enter():
        pl.semaphore_wait(barrier, len(peers))

    def first_sends():
        for w in "kv":
            at = W[w].at[z, x, own_rows("own")]
            send("w" + w + "y", at, at, yl_dev)
        for w in "kv":
            small_send(w, "own")
        for w in "kv":
            big_first(w, "own")

    def second_sends():
        for w in "kv":
            arrived("w" + w + "y", W[w].at[z, x, own_rows("par")])
            small_send(w, "par")
        for w in "kv":
            big_first(w, "par")

    def pass_on(j):
        for w in "kv":
            small_wait(w, j)
            big_send(w, j)

    def all_relayed(w):
        for n in "pm":
            for j in RELAYED[n]:
                relay_wait(w, n, j)


    step("enter", (enter,))
    step("first", (first_sends,), (send_cot, "k"), (partial_sums,), (send_cot_sib, "k"), (send_cot_sib, "v"))
    step("second", (second_sends,), (send_sums,))
    step("pass_m", (pass_on, "m"))
    step("pass_p", (pass_on, "p"))
    step("pass_2", (pass_on, "2"))
    step("send_cot_v", (send_cot, "v"), (load_t.wait,))
    step("proj0", (proj, "k", zs["0"], 0))
    step("relay_a", *[(relay, w, n, j) for n, j in ("p0", "mm") for w in "kv"])
    step("own_scale", (own_scale,))
    step("proj_cross0", (proj_cross, 0))
    step("relay_cot_k", (relay_cot, "k"))
    step("relay_b", *[(relay, w, n, j) for n, j in ("pp",) for w in "kv"])
    step("all_cots_k", (all_cots, "k"))
    step("transpose_k", (transpose, "k"))
    step("grads_k", (grads, "k"))
    step("relay_c", *[(relay, w, n, j) for n, j in ("m2",) for w in "kv"])
    step("g_far_k", (g_far, "k", 0), (g_far, "k", 1), (g_near, "k", 0), (g_near, "k", 1))
    step("row_scales", (row_scales,))
    step("relay_d", *[(relay, w, "p", j) for w in "kv" for j in "m2"], *[(relay, w, "m", j) for w in "kv" for j in "0p"])
    step("proj12", (proj, "k", zs["p"], 1), (proj, "k", zs["m"], 2), (proj_cross, 1), (proj_cross, 2))
    step("relay_cot_v", (relay_cot, "v"))
    step("g_relay_k", (g_relay, "k", 0), (g_relay, "k", 1))
    step("all_cots_v", (all_cots, "v"))
    step("transpose_v", (transpose, "v"))
    step("grads_v", (grads, "v"))
    step("g_far_v", (g_far, "v", 0), (g_far, "v", 1), (g_near, "v", 0), (g_near, "v", 1))
    step("all_w", (all_relayed, "k"), (all_relayed, "v"))
    step("proj3", (proj, "k", zs["2"], 3), (proj, "v", 0, 4), (proj_cross, 3))
    step("g_sum_k", (g_sum, "k", 0), (g_sum, "k", 1))
    step("projv", (proj, "v", 1, 5), (proj_cross, 4), (proj, "v", 2, 6), (proj_cross, 5))
    step("g_relay_v", (g_relay, "v", 0), (g_relay, "v", 1))
    step("projv", (proj, "v", 3, 7), (proj_cross, 6), (proj_cross, 7))
    step("scales", (plane_scales,))
    step("g_minor_k", (g_minor, "k"))
    step("all_scales", (all_scales,))
    step("input_grad", (input_grad,), (store, ig, ig_hbm))
    step("g_sum_v", (g_sum, "v", 0), (g_sum, "v", 1))
    step("proj_last_k", *[(proj_last, "k", zs[b], i) for i, b in enumerate("0pm2")], (store, kv_out.at[0], keys_hbm))
    step("proj_last_v", *[(proj_last, "v", i, 4 + i) for i in range(4)], (store, kv_out.at[1], vals_hbm))
    step("g_last_k", (g_last, "k", gk_hbm))
    step("g_minor_v", (g_minor, "v"))
    step("g_last_v", (g_last, "v", gv_hbm))
    for copy in outs:
        copy.wait()
    assert len(ids) <= N_SEM and len(local_ids) <= N_LOCAL
    for copy in started:
        copy.wait_send()


def hand_over(*refs):
    srcs, dsts, held, sem = refs[:5], refs[5:10], refs[10:15], refs[15]
    pieces = []
    for src, dst, mid in zip(srcs, dsts, held):
        rows = src.shape[-2] if len(src.shape) == 2 else 128
        for i in range(src.shape[0] if len(src.shape) == 3 else 1):
            for j in range(src.shape[-2] // rows):
                at = (pl.ds(j * rows, rows),)
                at = (i,) + at if len(src.shape) == 3 else at
                pieces.append((src.at[at], mid.at[at], dst.at[at]))
    loads, stores = [], []
    for i, (src, mid, dst) in enumerate(pieces):
        loads.append(pltpu.make_async_copy(src, mid, sem.at[0, i]))
        loads[-1].start()
    for i, (src, mid, dst) in enumerate(pieces):
        loads[i].wait()
        stores.append(pltpu.make_async_copy(mid, dst, sem.at[1, i]))
        stores[-1].start()
    for store in stores:
        store.wait()


def per_device(tokens, cot_key, cot_value, key_master, value_master):
    feat = tokens.shape[2]
    rows = key_master.shape[0]
    any_spec = pl.BlockSpec(memory_space=pl.ANY)
    vmem = pltpu.VMEM
    step = pl.pallas_call(
        kernel,
        out_shape=(
            jax.ShapeDtypeStruct(cot_key.shape, BF16),
            jax.ShapeDtypeStruct(cot_value.shape, BF16),
            jax.ShapeDtypeStruct(tokens.shape, BF16),
            jax.ShapeDtypeStruct(key_master.shape, F32),
            jax.ShapeDtypeStruct(value_master.shape, F32),
        ),
        in_specs=[any_spec] * 5,
        out_specs=(any_spec,) * 5,
        scratch_shapes=[
            vmem((2, 512, feat), BF16),
            vmem((2, 4, 128, 1024), BF16),
            vmem((2, 4, 128, 1024), BF16),
            vmem((1024, 1024), BF16),
            vmem((1024, 1024), BF16),
            vmem((2, rows, feat), F32),
            vmem((4, 2, rows, 128), F32),
            vmem((4, 4, 64, feat), BF16),
            vmem((4, 4, 64, feat), BF16),
            vmem((2, 4, 128, 256), F32),
            vmem((2, 4, 4, 64, feat), F32),
            vmem((2, 2, 2, 2, 32, feat), BF16),
            vmem((2, 2, 2, 2, 32, feat), BF16),
            vmem((2, 2, 2, 4, 32, feat), BF16),
            vmem((2, 2, 2, 4, 32, feat), BF16),
            vmem((2, 2, 3, 32, feat), BF16),
            vmem((2, 2, 3, 32, feat), BF16),
            vmem((2, 2, 32, feat), F32),
            vmem((2, 32, feat), BF16),
            vmem((2, 32, feat), BF16),
            vmem((2, 32, feat), F32),
            vmem((8, 2, 2, 128, 256), BF16),
            vmem((8, 2, 2, 128, 256), BF16),
            vmem((8, 2, 2, 128, 256), F32),
            vmem((8, 2, 128, 256), BF16),
            vmem((8, 2, 128, 256), BF16),
            vmem((2, 2, 128, 1024), BF16),
            vmem((2, 512, feat), BF16),
            vmem((8, 256), F32),
            vmem((8, 256), F32),
            vmem((4, 8, 256), F32),
            vmem((4, 8, 256), F32),
            vmem((2, 1024, 256), BF16),
            pltpu.SemaphoreType.DMA((N_LOCAL,)),
            pltpu.SemaphoreType.DMA((N_SEM,)),
            pltpu.SemaphoreType.DMA((N_SEM,)),
        ],
        compiler_params=pltpu.CompilerParams(
            collective_id=0, has_side_effects=True, vmem_limit_bytes=60 * 2**20
        ),
        cost_estimate=pl.CostEstimate(flops=16 * 10**9, bytes_accessed=10**7, transcendentals=0),
    )(tokens, cot_key, cot_value, key_master, value_master)
    return pl.pallas_call(
        hand_over,
        out_shape=tuple(jax.ShapeDtypeStruct(a.shape, a.dtype) for a in step),
        in_specs=[any_spec] * 5,
        out_specs=(any_spec,) * 5,
        scratch_shapes=[vmem(a.shape, a.dtype) for a in step] + [pltpu.SemaphoreType.DMA((2, 16))],
        compiler_params=pltpu.CompilerParams(vmem_limit_bytes=60 * 2**20),
    )(*step)


def solution(mesh):
    in_specs = (
        P(None, "dp", "mp"),
        P(None, ("dp", "mp"), None),
        P(None, ("dp", "mp"), None),
        P("dp", "mp"),
        P("dp", "mp"),
    )
    out_specs = (
        P(None, ("dp", "mp"), None),
        P(None, ("dp", "mp"), None),
        P(None, "dp", "mp"),
        P("dp", "mp"),
        P("dp", "mp"),
    )
    return jax.shard_map(
        per_device, mesh=mesh, in_specs=in_specs, out_specs=out_specs, check_vma=False
    )
```
